256 devices in a mesh: gx: 8 (over y, x_lo), gy: 32 (over x_hi, z, core).
Axes of the slice: x: 4 (x_hi: 2, x_lo: 2; x = x_hi * 2 + x_lo), y: 4, z: 8, core: 2. Of those that a mesh axis runs over, the one named last changes fastest.
Arguments:
- pressure: float32 [28, 1024, 1024], P(None, 'gy', 'gx'), may hold values from -6 to 6
- previous: float32 [28, 1024, 1024], P(None, 'gy', 'gx'), may hold values from -6 to 6
- branch_state: float32 [28, 1024, 1024], P(None, 'gy', 'gx'), may hold values from -6 to 6
- wall_mask: int32 [28, 1024, 1024], P(None, 'gy', 'gx'), may hold values 0 or 1
- material: int32 [28, 1024, 1024], P(None, 'gy', 'gx'), may hold values from 0 to 7
- ghost_low: float32 [1024, 1024], P('gy', 'gx'), may hold values from -6 to 6
- ghost_high: float32 [1024, 1024], P('gy', 'gx'), may hold values from -6 to 6
- wall_table: float32 [4, 8], replicated, may hold values from 0.05 to 3, as said below
Outputs:
- final_pressure: float32 [28, 1024, 1024], P(None, 'gy', 'gx')
- final_state: float32 [28, 1024, 1024], P(None, 'gy', 'gx')
The draws below stay inside these ranges and needn't reach their ends.
Inputs may be any that keep to these rules, and one draw needn't show every extreme that they name: `wall_table`: row 0 lies in 0.05 to 3, rows 1 to 3 in 0.05 to 1.
All inputs are finite; a program needn't handle non-finite values. No bound on the sum of `wall_mask` on one device may be relied on, other than what follows from the above.
Results may differ from the reference program's by a relative error of at most 0.00002.
Values sent between devices are 32-bit elements; how exact they have to be, the bound alone decides.
A program may use at most 64 MiB of HBM per device.

```python
import jax
import jax.numpy as jnp

NZ = 28
ITERS = 8
MATERIALS = 8
NX = 1024
NY = 1024


def draw_wall_table(key, part):
    key = jax.random.fold_in(key, 11)
    keys = jax.random.split(key, 4)
    loss = jnp.exp(jax.random.uniform(keys[0], (1, MATERIALS), jnp.float32, jnp.log(0.1), jnp.log(2.0)))
    weight = jax.random.uniform(keys[1], (1, MATERIALS), jnp.float32, 0.1, 0.6)
    decay = jax.random.uniform(keys[2], (1, MATERIALS), jnp.float32, 0.3, 0.95)
    couple = jax.random.uniform(keys[3], (1, MATERIALS), jnp.float32, 0.2, 1.0)
    rest = jnp.concatenate([weight, decay, couple], axis=0)
    return jnp.concatenate([loss, rest], axis=0)


def set_ends(values, stream_key, smallest, largest):
    spot = [jax.random.randint(jax.random.fold_in(stream_key, axis), (), 0, length) for axis, length in enumerate(values.shape)]
    longest = values.shape.index(max(values.shape))
    beside = spot[:longest] + [(spot[longest] + 1) % values.shape[longest]] + spot[longest + 1:]
    return values.at[tuple(spot)].set(smallest).at[tuple(beside)].set(largest)


def steps_of(stream_key, dims, cuts, least, largest):
    loudness, own = 1.0, jax.random.fold_in(stream_key, 6)
    for axis_at, blocks in cuts:
        draws = jnp.exp(jax.random.uniform(jax.random.fold_in(own, axis_at), (blocks,), jnp.float32, least / len(cuts), largest / len(cuts)))
        loudness = loudness * jnp.repeat(draws, dims[axis_at] // blocks).reshape([-1 if axis == axis_at else 1 for axis in range(len(dims))])
    return loudness


def noise(stream_key, extent, scale, reach, pieces=(), held_as=jnp.bfloat16):
    factor_of = steps_of(stream_key, extent, pieces, -0.22, 0.18) if pieces else 1.0
    result = jax.random.normal(stream_key, extent, jnp.float32) * scale * factor_of
    return jnp.minimum(jnp.maximum(result, -reach), reach).astype(held_as)


def setup_inputs(seed: int = 0) -> dict:
    arg_keys = jax.random.split(jax.random.key(seed), 9)
    pressure = noise(arg_keys[0], (NZ, NY, NX), 1.0, 6.0, ((1, 32), (2, 8)), jnp.float32)
    previous = noise(arg_keys[1], (NZ, NY, NX), 1.0, 6.0, ((1, 32), (2, 8)), jnp.float32)
    branch_state = noise(arg_keys[2], (NZ, NY, NX), 1.0, 6.0, ((1, 32), (2, 8)), jnp.float32)
    wall_mask = set_ends((jax.random.randint(arg_keys[3], (NZ, NY, NX), 0, 4) < 1).astype(jnp.int32), jax.random.fold_in(arg_keys[3], 1), 0, 1)
    material = set_ends(jax.random.randint(arg_keys[4], (NZ, NY, NX), 0, MATERIALS), jax.random.fold_in(arg_keys[4], 1), 0, MATERIALS - 1).astype(jnp.int32)
    ghost_low = noise(arg_keys[5], (NY, NX), 1.0, 6.0, ((0, 32), (1, 8)), jnp.float32)
    ghost_high = noise(arg_keys[6], (NY, NX), 1.0, 6.0, ((0, 32), (1, 8)), jnp.float32)
    wall_table = draw_wall_table(jax.random.fold_in(arg_keys[8], 71), 0)
    return {"pressure": pressure, "previous": previous, "branch_state": branch_state, "wall_mask": wall_mask, "material": material, "ghost_low": ghost_low, "ghost_high": ghost_high, "wall_table": wall_table}


courant_sq = 0.33


def laplace(field, low, high):
    side_y = jnp.pad(field, ((0, 0), (1, 1), (0, 0)))
    side_x = jnp.pad(field, ((0, 0), (0, 0), (1, 1)))
    below = jnp.concatenate([low[None], field[:-1]], axis=0)
    above = jnp.concatenate([field[1:], high[None]], axis=0)
    return (side_y[:, 2:] + side_y[:, :-2]) + (side_x[:, :, 2:] + side_x[:, :, :-2]) + (below + above) - 6.0 * field


def reference(pressure, previous, branch_state, wall_mask, material, ghost_low, ghost_high, wall_table):
    maskf = wall_mask.astype(jnp.float32)
    walls = wall_mask == 1
    beta = jnp.take(wall_table[0], material) * maskf
    weight = jnp.take(wall_table[1], material) * maskf
    decay = jnp.take(wall_table[2], material)
    couple = jnp.take(wall_table[3], material)
    field, older, state = pressure, previous, branch_state
    for step in range(ITERS):
        source = 2.0 * field - older + courant_sq * laplace(field, ghost_low, ghost_high)
        newer = (source + beta * older - weight * state) / (1.0 + beta)
        state = jnp.where(walls, decay * state + couple * (newer - older), state)
        older, field = field, newer
    return field, state
```

```python
import jax
import jax.numpy as jnp
from jax import lax
from jax.experimental import pallas as pl
from jax.experimental.pallas import tpu as pltpu
from jax.sharding import PartitionSpec as P

ITERS = 8
NZ = 28
ROWS = 32
LANES = 128
H = 8
GROUPS = 4
PLANES = 7
BUF = ROWS + 4 * H
TALL = ROWS + 2 * H
COURANT = 0.33
K0 = (2.0 - 6.0 * COURANT) / COURANT
K1 = 2.0 / COURANT
AIR = 8
OUTSIDE = 9
OFFSET = (0, 8, 64, 72)
MESH = pl.DeviceIdType.MESH
F32 = jnp.float32


def roll(value, shift):
    shift %= LANES
    return value if shift == 0 else pltpu.roll(value, shift, axis=1)


def lane_ids():
    return lax.broadcasted_iota(jnp.int32, (8, LANES), 1)


def class_tables(table):
    lane = lane_ids()
    rows = []
    for row, air in ((0, 0.0), (1, 0.0), (2, 1.0), (3, 0.0)):
        picked = jnp.full((8, LANES), air, F32)
        for index in range(8):
            picked = jnp.where(lane == index, table[row, index], picked)
        rows.append(picked)
    loss = 1.0 / (1.0 + rows[0])
    source = jnp.where(lane == OUTSIDE, 0.0, COURANT * loss)
    return (source, rows[1] * loss, rows[2], rows[3])


def look_up(tables, cells):
    index = cells.astype(jnp.int32)
    return [jnp.take_along_axis(t, index, axis=1, mode="promise_in_bounds") for t in tables]


def cell_step(centre, around, older, state, source, weight, decay, couple):
    moved = source * (around + K0 * centre - K1 * older) - weight * state
    return older + moved, decay * state + couple * moved


def kernel(
    n_x, n_y,
    p_in, q_in, v_in, mask_in, mat_in, low_in, high_in, table,
    p_out, v_out,
    field_a, field_b, field_c, state_a, state_b, cls, coef, mask, mat,
    m_left, m_right, r_left, r_right,
    s_field_a, s_field_b, s_field_c, s_state_a, s_state_b, s_coef, s_ghost, edge,
    load_sem, send_sem, recv_sem,
):
    field, state = (field_a, field_b, field_c), (state_a, state_b)
    s_field, s_state = (s_field_a, s_field_b, s_field_c), (s_state_a, s_state_b)
    gx, gy = lax.axis_index("gx"), lax.axis_index("gy")

    def there(dx, dy):
        x, y = gx + dx, gy + dy
        return (x >= 0) & (x < n_x) & (y >= 0) & (y < n_y)

    around = [(dx, dy) for dx in (-1, 0, 1) for dy in (-1, 0, 1) if dx or dy]
    barrier = pltpu.get_barrier_semaphore()
    count = jnp.int32(0)
    for dx, dy in around:
        ok = there(dx, dy)
        count = count + ok.astype(jnp.int32)

        @pl.when(ok)
        def _():
            pl.semaphore_signal(barrier, inc=1, device_id=(gx + dx, gy + dy), device_id_type=MESH)

    own = pl.ds(2 * H, ROWS)
    loads = [
        pltpu.make_async_copy(src, dst, load_sem.at[i])
        for i, (src, dst) in enumerate(
            [
                (p_in, field[0].at[pl.ds(1, NZ), own]),
                (q_in, field[1].at[pl.ds(1, NZ), own]),
                (v_in, state[0].at[:, own]),
                (mask_in, mask),
                (mat_in, mat),
                (low_in, field[0].at[0, own]),
                (high_in, field[0].at[NZ + 1, own]),
            ]
        )
    ]
    for load in loads:
        load.start()

    lane = lane_ids()
    place = lane % 16
    tables = class_tables(table)
    for load in loads:
        load.wait()

    @pl.loop(0, NZ)
    def _(z):
        for k in range(4):
            rows = pl.ds(8 * k, 8)
            wall = mask[z, rows, :] == 1
            cls[z, pl.ds(16 + 8 * k, 8), :] = jnp.where(wall, mat[z, rows, :], AIR).astype(F32)

    def pack(out, first, spare, ghost_shift):
        @pl.loop(0, PLANES)
        def _(j):
            for k in range(4):
                rows = pl.ds(16 + 8 * k, 8)
                total = jnp.zeros((8, LANES), F32)
                for a in range(4):
                    for g in range(GROUPS):
                        z = 7 * g + j
                        if a == 0:
                            value = field[0][z + 1, rows, :]
                        elif a == 1:
                            value = field[1][z + 1, rows, :]
                        elif a == 2:
                            value = state[0][z, rows, :]
                        else:
                            value = cls[z, rows, :]
                        to = OFFSET[a] + 16 * g
                        total = jnp.where((lane >= to) & (lane < to + 8), roll(value, to - first), total)
                out[j, pl.ds(8 + 8 * k, 8), :] = total

        for j in range(PLANES):
            at = first + j + ghost_shift
            for k in range(4):
                rows, into = pl.ds(16 + 8 * k, 8), pl.ds(8 + 8 * k, 8)
                low_at, high_at = OFFSET[1] + spare, OFFSET[1] + 48 + spare
                value = out[j, into, :]
                value = jnp.where(lane == low_at, roll(field[0][0, rows, :], low_at - at), value)
                value = jnp.where(lane == high_at, roll(field[0][NZ + 1, rows, :], high_at - at), value)
                out[j, into, :] = value

    pack(m_left, 0, 7, 0)
    pack(m_right, LANES - 8, 0, 1)

    pl.semaphore_wait(barrier, count)

    transfers = []

    def transfer(src, dst, dx, dy):
        i = len(transfers)
        copy = pltpu.make_async_remote_copy(
            src_ref=src, dst_ref=dst, send_sem=send_sem.at[i], recv_sem=recv_sem.at[i],
            device_id=(gx + dx, gy + dy), device_id_type=MESH,
        )
        transfers.append((copy, dx, dy))

    for dx, message, into in ((1, m_right, r_left), (-1, m_left, r_right)):
        transfer(message.at[:, pl.ds(8, ROWS)], into.at[:, pl.ds(8, ROWS)], dx, 0)
    for dy, main_from, main_to, part_from, part_to in ((1, 40, 8, 32, 0), (-1, 16, 48, 8, 40)):
        for dx, message, into in ((1, m_right, r_left), (-1, m_left, r_right)):
            transfer(message.at[:, pl.ds(part_from, 8)], into.at[:, pl.ds(part_to, 8)], dx, dy)
        src, dst = pl.ds(main_from, 8), pl.ds(main_to, 8)
        transfer(field[0].at[:, src], field[0].at[:, dst], 0, dy)
        transfer(field[1].at[pl.ds(1, NZ), src], field[1].at[pl.ds(1, NZ), dst], 0, dy)
        transfer(state[0].at[:, src], state[0].at[:, dst], 0, dy)
        transfer(cls.at[:, src], cls.at[:, dst], 0, dy)
        for message in (m_left, m_right):
            transfer(message.at[:, pl.ds(part_from, 8)], message.at[:, pl.ds(part_to, 8)], 0, dy)

    for copy, dx, dy in transfers:

        @pl.when(there(dx, dy))
        def _():
            copy.start()

    nothing = jnp.where((lane >= 64) & (place >= 8), float(OUTSIDE), 0.0).astype(F32)

    def blank(ref, first, rows):
        @pl.loop(0, PLANES)
        def _(j):
            for k in range(rows // 8):
                ref[j, pl.ds(first + 8 * k, 8), :] = nothing

    for dy, main, part in ((-1, 8, 0), (1, 48, 40)):

        @pl.when(jnp.logical_not(there(0, dy)))
        def _():
            rows = pl.ds(main, 8)
            zero = jnp.zeros((8, LANES), F32)
            field[0][0, rows, :] = zero
            field[0][NZ + 1, rows, :] = zero

            @pl.loop(0, NZ)
            def _(z):
                field[0][z + 1, rows, :] = zero
                field[1][z + 1, rows, :] = zero
                state[0][z, rows, :] = zero
                cls[z, rows, :] = jnp.full((8, LANES), float(OUTSIDE), F32)

            blank(m_left, part, 8)
            blank(m_right, part, 8)

        for dx, ref in ((-1, r_left), (1, r_right)):

            @pl.when(there(dx, 0) & jnp.logical_not(there(0, dy)))
            def _():
                blank(ref, part, 8)

    for dx, ref in ((-1, r_left), (1, r_right)):

        @pl.when(jnp.logical_not(there(dx, 0)))
        def _():
            blank(ref, 0, TALL)

    def coefficients(k):
        @pl.loop(0, NZ)
        def _(z):
            rows = pl.ds(8 + 8 * k, 8)
            for i, value in enumerate(look_up(tables, cls[z, rows, :])):
                coef[i, z, rows, :] = value

    for k in (1, 2, 3, 4):
        coefficients(k)

    for copy, dx, dy in transfers:

        @pl.when(there(-dx, -dy))
        def _():
            copy.wait_recv()

    for copy, dx, dy in transfers:

        @pl.when(there(dx, dy))
        def _():
            copy.wait_send()

    coefficients(0)
    coefficients(5)
    for k in range(6):
        rows = pl.ds(8 + 8 * k, 8)
        for plane in (0, NZ + 1):
            ghost = field[0][plane, rows, :]
            field[1][plane, rows, :] = ghost
            field[2][plane, rows, :] = ghost

    side, half = lane >= 64, place >= 8

    def gather_strip(a, j, rows):
        at = OFFSET[a]
        lower = jnp.where(half, roll(m_left[j, rows, :], 8 - at), roll(r_left[j, rows, :], -at))
        upper = jnp.where(half, roll(r_right[j, rows, :], 72 - at), roll(m_right[j, rows, :], 64 - at))
        return jnp.where(side, upper, lower)

    @pl.loop(0, PLANES)
    def _(j):
        for k in range(6):
            rows, into = pl.ds(8 * k, 8), pl.ds(8 + 8 * k, 8)
            s_field[0][j + 1, into, :] = gather_strip(0, j, rows)
            s_field[1][j + 1, into, :] = gather_strip(1, j, rows)
            s_state[0][j, into, :] = gather_strip(2, j, rows)
            for i, value in enumerate(look_up(tables, gather_strip(3, j, rows))):
                s_coef[i, j, into, :] = value

    for k in range(6):
        rows = pl.ds(8 * k, 8)
        total = jnp.zeros((8, LANES), F32)
        for j in range(PLANES):
            for ref, spare, to in ((r_left, 0, 1), (m_left, 7, 8), (m_right, 0, 65), (r_right, 7, 72)):
                value = roll(ref[j, rows, :], to + j - OFFSET[1] - spare)
                total = jnp.where((lane == to + j) | (lane == to + j + 48), value, total)
        s_ghost[pl.ds(8 + 8 * k, 8), :] = total

    group = (lane // 16) % 4

    def strip_ends(now):
        for k in range(6):
            rows = pl.ds(8 + 8 * k, 8)
            ghost = s_ghost[rows, :]
            s_field[now][0, rows, :] = jnp.where(group == 0, ghost, roll(s_field[now][PLANES, rows, :], 16))
            s_field[now][PLANES + 1, rows, :] = jnp.where(group == 3, ghost, roll(s_field[now][1, rows, :], -16))

    strip_ends(0)
    mark = place == 6

    def column(ref, plane, blocks):
        return [
            (ref[plane, pl.ds(8 + 8 * k, 8), :], ref[plane, pl.ds(7 + 8 * k, 8), :] + ref[plane, pl.ds(9 + 8 * k, 8), :])
            for k in blocks
        ]

    def strip_step(p, q, out, v, v_out, blocks):
        @pl.loop(0, PLANES, unroll=7)
        def _(j):
            done = []
            for k, (centre, y_sum) in zip(blocks, column(p, j + 1, blocks)):
                rows = pl.ds(8 + 8 * k, 8)
                edge[j, rows, :] = jnp.where(mark, roll(centre, -66), centre)
                total = (roll(centre, 1) + roll(centre, -1)) + y_sum + (p[j, rows, :] + p[j + 2, rows, :])
                done.append((rows,) + cell_step(
                    centre, total, q[j + 1, rows, :], v[j, rows, :], *[s_coef[i, j, rows, :] for i in range(4)],
                ))
            for rows, newer, filt in done:
                out[j + 1, rows, :] = newer
                v_out[j, rows, :] = filt

    first_lane, last_lane = lane == 0, lane == LANES - 1

    def main_step(p, q, v, blocks, store):
        for g in range(GROUPS):

            @pl.loop(0, PLANES, unroll=7)
            def _(j):
                z = 7 * g + j
                done = []
                for k, (centre, y_sum) in zip(blocks, column(p, z + 1, blocks)):
                    rows = pl.ds(8 + 8 * k, 8)
                    beside = roll(edge[j, rows, :], -(16 * g + 7))
                    total = (
                        (jnp.where(first_lane, beside, roll(centre, 1)) + jnp.where(last_lane, beside, roll(centre, -1)))
                        + y_sum
                        + (p[z, rows, :] + p[z + 2, rows, :])
                    )
                    done.append((k,) + cell_step(
                        centre, total, q[z + 1, rows, :], v[z, rows, :], *[coef[i, z, rows, :] for i in range(4)],
                    ))
                for k, newer, filt in done:
                    store(z, k, newer, filt)

    every, inner = range(6), range(1, 5)
    for step in range(ITERS):
        now, old, new = [(0, 1, 2), (2, 0, 1), (1, 2, 0)][step % 3]
        v, v_new = state[step % 2], state[1 - step % 2]
        last = step == ITERS - 1
        strip_step(s_field[now], s_field[old], s_field[new], s_state[step % 2], s_state[1 - step % 2], inner if last else every)
        if not last:
            strip_ends(new)

        def store(z, k, newer, filt):
            rows = pl.ds(8 + 8 * k, 8)
            field[new][z + 1, rows, :] = newer
            v_new[z, rows, :] = filt

        def store_out(z, k, newer, filt):
            rows = pl.ds(8 * k - 8, 8)
            p_out[z, rows, :] = newer
            v_out[z, rows, :] = filt

        main_step(field[now], field[old], v, inner if last else every, store_out if last else store)


def solution(mesh):
    n_x, n_y = mesh.shape["gx"], mesh.shape["gy"]

    def body(*args):
        hbm = pl.BlockSpec(memory_space=pltpu.HBM)
        vmem = pl.BlockSpec(memory_space=pltpu.VMEM)
        big = (NZ, BUF, LANES)
        strip = (PLANES, BUF, LANES)
        message = pltpu.VMEM((PLANES, TALL, LANES), F32)
        tall, s_tall = (pltpu.VMEM((n + 2, BUF, LANES), F32) for n in (NZ, PLANES))
        n_transfers = 18
        return pl.pallas_call(
            lambda *refs: kernel(n_x, n_y, *refs),
            out_shape=[pltpu.VMEM((NZ, ROWS, LANES), F32)] * 2,
            in_specs=[hbm] * 7 + [pl.BlockSpec(memory_space=pltpu.SMEM)],
            out_specs=[vmem] * 2,
            scratch_shapes=[
                tall, tall, tall,
                pltpu.VMEM(big, F32),
                pltpu.VMEM(big, F32),
                pltpu.VMEM(big, F32),
                pltpu.VMEM((4,) + big, F32),
                pltpu.VMEM((NZ, ROWS, LANES), jnp.int32),
                pltpu.VMEM((NZ, ROWS, LANES), jnp.int32),
                message, message, message, message,
                s_tall, s_tall, s_tall,
                pltpu.VMEM(strip, F32),
                pltpu.VMEM(strip, F32),
                pltpu.VMEM((4,) + strip, F32),
                pltpu.VMEM((BUF, LANES), F32),
                pltpu.VMEM(strip, F32),
                pltpu.SemaphoreType.DMA((7,)),
                pltpu.SemaphoreType.DMA((n_transfers,)),
                pltpu.SemaphoreType.DMA((n_transfers,)),
            ],
            compiler_params=pltpu.CompilerParams(
                collective_id=1, has_side_effects=True, vmem_limit_bytes=62 * 1024 * 1024
            ),
        )(*args)

    spec = P(None, "gy", "gx")
    return jax.shard_map(
        body,
        mesh=mesh,
        in_specs=(spec,) * 5 + (P("gy", "gx"),) * 2 + (P(),),
        out_specs=(spec, spec),
        check_vma=False,
    )
```

```python
import jax
import jax.numpy as jnp
from jax import lax
from jax.experimental import pallas as pl
from jax.experimental.pallas import tpu as pltpu
from jax.sharding import PartitionSpec as P

ITERS = 8
NZ = 28
ROWS = 32
LANES = 128
H = 8
GROUPS = 4
PLANES = 7
BUF = ROWS + 4 * H
TALL = ROWS + 2 * H
COURANT = 0.33
K0 = (2.0 - 6.0 * COURANT) / COURANT
K1 = 2.0 / COURANT
AIR = 8
OUTSIDE = 9
OFFSET = (0, 8, 64, 72)
MESH = pl.DeviceIdType.MESH
F32 = jnp.float32


def roll(value, shift):
    shift %= LANES
    return value if shift == 0 else pltpu.roll(value, shift, axis=1)


def lane_ids():
    return lax.broadcasted_iota(jnp.int32, (8, LANES), 1)


def class_tables(table):
    lane = lane_ids()
    rows = []
    for row, air in ((0, 0.0), (1, 0.0), (2, 1.0), (3, 0.0)):
        picked = jnp.full((8, LANES), air, F32)
        for index in range(8):
            picked = jnp.where(lane == index, table[row, index], picked)
        rows.append(picked)
    loss = 1.0 / (1.0 + rows[0])
    source = jnp.where(lane == OUTSIDE, 0.0, COURANT * loss)
    return (source, rows[1] * loss, rows[2], rows[3])


def look_up(tables, cells):
    index = cells.astype(jnp.int32)
    return [jnp.take_along_axis(t, index, axis=1, mode="promise_in_bounds") for t in tables]


def cell_step(centre, around, older, state, source, weight, decay, couple):
    moved = source * (around + K0 * centre - K1 * older) - weight * state
    return older + moved, decay * state + couple * moved


def kernel(
    n_x, n_y,
    p_in, q_in, v_in, mask_in, mat_in, low_in, high_in, table,
    p_out, v_out,
    field_a, field_b, state_a, cls, coef, mask, mat,
    m_left, m_right, r_left, r_right,
    s_field_a, s_field_b, s_state_a, s_coef, s_ghost, edge,
    load_sem, send_sem, recv_sem,
):
    field, state = (field_a, field_b), (state_a,)
    s_field, s_state = (s_field_a, s_field_b), (s_state_a,)
    gx, gy = lax.axis_index("gx"), lax.axis_index("gy")

    def there(dx, dy):
        x, y = gx + dx, gy + dy
        return (x >= 0) & (x < n_x) & (y >= 0) & (y < n_y)

    around = [(dx, dy) for dx in (-1, 0, 1) for dy in (-1, 0, 1) if dx or dy]
    barrier = pltpu.get_barrier_semaphore()
    count = jnp.int32(0)
    for dx, dy in around:
        ok = there(dx, dy)
        count = count + ok.astype(jnp.int32)

        @pl.when(ok)
        def _():
            pl.semaphore_signal(barrier, inc=1, device_id=(gx + dx, gy + dy), device_id_type=MESH)

    own = pl.ds(2 * H, ROWS)
    loads = [
        pltpu.make_async_copy(src, dst, load_sem.at[i])
        for i, (src, dst) in enumerate(
            [
                (p_in, field[0].at[pl.ds(1, NZ), own]),
                (q_in, field[1].at[pl.ds(1, NZ), own]),
                (v_in, state[0].at[:, own]),
                (mask_in, mask),
                (mat_in, mat),
                (low_in, field[0].at[0, own]),
                (high_in, field[0].at[NZ + 1, own]),
            ]
        )
    ]
    for load in loads:
        load.start()

    lane = lane_ids()
    place = lane % 16
    tables = class_tables(table)
    for load in loads:
        load.wait()

    @pl.loop(0, NZ, unroll=7)
    def _(z):
        for k in range(4):
            rows = pl.ds(8 * k, 8)
            wall = mask[z, rows, :] == 1
            cls[z, pl.ds(16 + 8 * k, 8), :] = jnp.where(wall, mat[z, rows, :], AIR).astype(F32)

    def merge(bit, low, high):
        return jnp.where((lane & bit) != 0, high, low)

    def pack(out, first, spare, ghost_shift):
        def column(a, z, rows):
            ref, plane = ((field[0], z + 1), (field[1], z + 1), (state[0], z), (cls, z))[a]
            return ref[plane, rows, :]

        for j in range(PLANES):
            at = first + j + ghost_shift
            low_at, high_at = OFFSET[1] + spare, OFFSET[1] + 48 + spare
            for k in range(4):
                rows = pl.ds(16 + 8 * k, 8)
                parts = [
                    [roll(column(a, 7 * g + j, rows), OFFSET[a] + 16 * g - first) for g in range(GROUPS)]
                    for a in range(4)
                ]
                parts[1][0] = jnp.where(lane == low_at, roll(field[0][0, rows, :], low_at - at), parts[1][0])
                parts[1][3] = jnp.where(lane == high_at, roll(field[0][NZ + 1, rows, :], high_at - at), parts[1][3])
                halves = []
                for a in (0, 2):
                    g = [merge(8, parts[a][g], parts[a + 1][g]) for g in range(GROUPS)]
                    halves.append(merge(32, merge(16, g[0], g[1]), merge(16, g[2], g[3])))
                out[j, pl.ds(8 + 8 * k, 8), :] = merge(64, halves[0], halves[1])

    pack(m_left, 0, 7, 0)
    pack(m_right, LANES - 8, 0, 1)

    pl.semaphore_wait(barrier, count)

    transfers = []

    def transfer(src, dst, dx, dy, heavy=False):
        i = len(transfers)
        copy = pltpu.make_async_remote_copy(
            src_ref=src, dst_ref=dst, send_sem=send_sem.at[i], recv_sem=recv_sem.at[i],
            device_id=(gx + dx, gy + dy), device_id_type=MESH,
        )
        transfers.append((copy, dx, dy, heavy))

    for dx, message, into in ((1, m_right, r_left), (-1, m_left, r_right)):
        transfer(message.at[:, pl.ds(8, ROWS)], into.at[:, pl.ds(8, ROWS)], dx, 0)
    for dy, main_from, main_to, part_from, part_to in ((1, 40, 8, 32, 0), (-1, 16, 48, 8, 40)):
        for dx, message, into in ((1, m_right, r_left), (-1, m_left, r_right)):
            transfer(message.at[:, pl.ds(part_from, 8)], into.at[:, pl.ds(part_to, 8)], dx, dy)
        src, dst = pl.ds(main_from, 8), pl.ds(main_to, 8)
        transfer(field[0].at[:, src], field[0].at[:, dst], 0, dy)
        transfer(field[1].at[pl.ds(1, NZ), src], field[1].at[pl.ds(1, NZ), dst], 0, dy)
        transfer(state[0].at[:, src], state[0].at[:, dst], 0, dy)
        transfer(cls.at[:, src], cls.at[:, dst], 0, dy)
        for message in (m_left, m_right):
            transfer(message.at[:, pl.ds(part_from, 8)], message.at[:, pl.ds(part_to, 8)], 0, dy, dy > 0)

    def long_step(dy):
        return gy + max(dy, 0) == n_y // 2

    for copy, dx, dy, heavy in transfers:
        at_once = there(dx, dy)
        if heavy:
            at_once = at_once & jnp.logical_not(long_step(dy))

        @pl.when(at_once)
        def _():
            copy.start()

    nothing = jnp.where((lane >= 64) & (place >= 8), float(OUTSIDE), 0.0).astype(F32)

    def blank(ref, first, rows):
        @pl.loop(0, PLANES)
        def _(j):
            for k in range(rows // 8):
                ref[j, pl.ds(first + 8 * k, 8), :] = nothing

    for dy, main, part in ((-1, 8, 0), (1, 48, 40)):

        @pl.when(jnp.logical_not(there(0, dy)))
        def _():
            rows = pl.ds(main, 8)
            zero = jnp.zeros((8, LANES), F32)
            field[0][0, rows, :] = zero
            field[0][NZ + 1, rows, :] = zero

            @pl.loop(0, NZ)
            def _(z):
                field[0][z + 1, rows, :] = zero
                field[1][z + 1, rows, :] = zero
                state[0][z, rows, :] = zero
                cls[z, rows, :] = jnp.full((8, LANES), float(OUTSIDE), F32)

            blank(m_left, part, 8)
            blank(m_right, part, 8)

        for dx, ref in ((-1, r_left), (1, r_right)):

            @pl.when(there(dx, 0) & jnp.logical_not(there(0, dy)))
            def _():
                blank(ref, part, 8)

    for dx, ref in ((-1, r_left), (1, r_right)):

        @pl.when(jnp.logical_not(there(dx, 0)))
        def _():
            blank(ref, 0, TALL)

    def coefficients(blocks):
        @pl.loop(0, NZ, unroll=7)
        def _(z):
            for k in blocks:
                rows = pl.ds(8 + 8 * k, 8)
                for i, value in enumerate(look_up(tables, cls[z, rows, :])):
                    coef[i, z, rows, :] = value

    coefficients((1, 2, 3, 4))

    def receive(of_x):
        for copy, dx, dy, _ in transfers:
            if (dy == 0) == of_x:

                @pl.when(there(-dx, -dy))
                def _():
                    copy.wait_recv()

    receive(True)
    for copy, dx, dy, heavy in transfers:
        if heavy:

            @pl.when(there(dx, dy) & long_step(dy))
            def _():
                copy.start()

    receive(False)
    coefficients((0, 5))
    for k in range(6):
        rows = pl.ds(8 + 8 * k, 8)
        for plane in (0, NZ + 1):
            ghost = field[0][plane, rows, :]
            field[1][plane, rows, :] = ghost

    def gather_strip(a, j, rows):
        at = OFFSET[a]
        lower = merge(8, roll(r_left[j, rows, :], -at), roll(m_left[j, rows, :], 8 - at))
        upper = merge(8, roll(m_right[j, rows, :], 64 - at), roll(r_right[j, rows, :], 72 - at))
        return merge(64, lower, upper)

    @pl.loop(0, PLANES, unroll=7)
    def _(j):
        for k in range(6):
            rows, into = pl.ds(8 * k, 8), pl.ds(8 + 8 * k, 8)
            s_field[0][j + 1, into, :] = gather_strip(0, j, rows)
            s_field[1][j + 1, into, :] = gather_strip(1, j, rows)
            s_state[0][j, into, :] = gather_strip(2, j, rows)
            for i, value in enumerate(look_up(tables, gather_strip(3, j, rows))):
                s_coef[i, j, into, :] = value

    for k in range(6):
        rows = pl.ds(8 * k, 8)
        total = jnp.zeros((8, LANES), F32)
        for j in range(PLANES):
            for ref, spare, to in ((r_left, 0, 1), (m_left, 7, 8), (m_right, 0, 65), (r_right, 7, 72)):
                value = roll(ref[j, rows, :], to + j - OFFSET[1] - spare)
                total = jnp.where((lane == to + j) | (lane == to + j + 48), value, total)
        s_ghost[pl.ds(8 + 8 * k, 8), :] = total

    group = (lane // 16) % 4

    def strip_ends(ref):
        for k in range(6):
            rows = pl.ds(8 + 8 * k, 8)
            ghost = s_ghost[rows, :]
            ref[0, rows, :] = jnp.where(group == 0, ghost, roll(ref[PLANES, rows, :], 16))
            ref[PLANES + 1, rows, :] = jnp.where(group == 3, ghost, roll(ref[1, rows, :], -16))

    strip_ends(s_field[0])
    mark = place == 6


    def y_sum(ref, plane, k):
        return ref[plane, pl.ds(7 + 8 * k, 8), :] + ref[plane, pl.ds(9 + 8 * k, 8), :]

    def strip_step(p, q, blocks):
        for j in range(PLANES):
            done = []
            for k in blocks:
                rows = pl.ds(8 + 8 * k, 8)
                centre = p[j + 1, rows, :]
                edge[j, rows, :] = jnp.where(mark, roll(centre, -66), centre)
                total = (roll(centre, 1) + roll(centre, -1)) + y_sum(p, j + 1, k) + (p[j, rows, :] + p[j + 2, rows, :])
                done.append((rows,) + cell_step(
                    centre, total, q[j + 1, rows, :], s_state[0][j, rows, :], *[s_coef[i, j, rows, :] for i in range(4)],
                ))
            for rows, newer, filt in done:
                q[j + 1, rows, :] = newer
                s_state[0][j, rows, :] = filt

    first_lane, last_lane = lane == 0, lane == LANES - 1

    def main_step(p, q, blocks, store):
        def group_step(g):
            shift = LANES - 7 - 16 * g
            for j in range(PLANES):
                z = 7 * g + j
                done = []
                for k in blocks:
                    rows = pl.ds(8 + 8 * k, 8)
                    centre = p[z + 1, rows, :]
                    beside = pltpu.roll(edge[j, rows, :], shift, axis=1)
                    total = (
                        (jnp.where(first_lane, beside, roll(centre, 1)) + jnp.where(last_lane, beside, roll(centre, -1)))
                        + y_sum(p, z + 1, k)
                        + (p[z, rows, :] + p[z + 2, rows, :])
                    )
                    done.append((k,) + cell_step(
                        centre, total, q[z + 1, rows, :], state[0][z, rows, :], *[coef[i, z, rows, :] for i in range(4)],
                    ))
                for k, newer, filt in done:
                    store(z, k, newer, filt)

        for g in range(GROUPS):
            group_step(g)

    every, inner = range(6), range(1, 5)

    def step(p, q, sp, sq):
        strip_step(sp, sq, every)
        strip_ends(sq)

        def store(z, k, newer, filt):
            rows = pl.ds(8 + 8 * k, 8)
            q[z + 1, rows, :] = newer
            state[0][z, rows, :] = filt

        main_step(p, q, every, store)

    for copy, dx, dy, _ in transfers:

        @pl.when(there(dx, dy))
        def _():
            copy.wait_send()

    @pl.loop(0, ITERS // 2 - 1)
    def _(pair):
        step(field[0], field[1], s_field[0], s_field[1])
        step(field[1], field[0], s_field[1], s_field[0])

    step(field[0], field[1], s_field[0], s_field[1])
    strip_step(s_field[1], s_field[0], inner)

    def store_out(z, k, newer, filt):
        rows = pl.ds(8 * k - 8, 8)
        p_out[z, rows, :] = newer
        v_out[z, rows, :] = filt

    main_step(field[1], field[0], inner, store_out)


def solution(mesh):
    n_x, n_y = mesh.shape["gx"], mesh.shape["gy"]

    def body(*args):
        hbm = pl.BlockSpec(memory_space=pltpu.HBM)
        vmem = pl.BlockSpec(memory_space=pltpu.VMEM)
        big = (NZ, BUF, LANES)
        strip = (PLANES, BUF, LANES)
        message = pltpu.VMEM((PLANES, TALL, LANES), F32)
        tall, s_tall = (pltpu.VMEM((n + 2, BUF, LANES), F32) for n in (NZ, PLANES))
        n_transfers = 18
        return pl.pallas_call(
            lambda *refs: kernel(n_x, n_y, *refs),
            out_shape=[pltpu.VMEM((NZ, ROWS, LANES), F32)] * 2,
            in_specs=[hbm] * 7 + [pl.BlockSpec(memory_space=pltpu.SMEM)],
            out_specs=[vmem] * 2,
            scratch_shapes=[
                tall, tall,
                pltpu.VMEM(big, F32),
                pltpu.VMEM(big, F32),
                pltpu.VMEM((4,) + big, F32),
                pltpu.VMEM((NZ, ROWS, LANES), jnp.int32),
                pltpu.VMEM((NZ, ROWS, LANES), jnp.int32),
                message, message, message, message,
                s_tall, s_tall,
                pltpu.VMEM(strip, F32),
                pltpu.VMEM((4,) + strip, F32),
                pltpu.VMEM((BUF, LANES), F32),
                pltpu.VMEM(strip, F32),
                pltpu.SemaphoreType.DMA((7,)),
                pltpu.SemaphoreType.DMA((n_transfers,)),
                pltpu.SemaphoreType.DMA((n_transfers,)),
            ],
            compiler_params=pltpu.CompilerParams(
                collective_id=1, has_side_effects=True, vmem_limit_bytes=62 * 1024 * 1024
            ),
        )(*args)

    spec = P(None, "gy", "gx")
    return jax.shard_map(
        body,
        mesh=mesh,
        in_specs=(spec,) * 5 + (P("gy", "gx"),) * 2 + (P(),),
        out_specs=(spec, spec),
        check_vma=False,
    )
```

```python
import jax
import jax.numpy as jnp
from jax import lax
from jax.experimental import pallas as pl
from jax.experimental.pallas import tpu as pltpu
from jax.sharding import PartitionSpec as P

ITERS = 8
NZ = 28
ROWS = 32
LANES = 128
H = 8
GROUPS = 4
PLANES = 7
BUF = ROWS + 4 * H
TALL = ROWS + 2 * H
COURANT = 0.33
K0 = (2.0 - 6.0 * COURANT) / COURANT
K1 = 2.0 / COURANT
AIR = 8
OUTSIDE = 9
OFFSET = (0, 8, 64, 72)
MESH = pl.DeviceIdType.MESH
F32 = jnp.float32


def roll(value, shift):
    shift %= LANES
    return value if shift == 0 else pltpu.roll(value, shift, axis=1)


def lane_ids():
    return lax.broadcasted_iota(jnp.int32, (8, LANES), 1)


def class_tables(table):
    lane = lane_ids()
    rows = []
    for row, air in ((0, 0.0), (1, 0.0), (2, 1.0), (3, 0.0)):
        picked = jnp.full((8, LANES), air, F32)
        for index in range(8):
            picked = jnp.where(lane == index, table[row, index], picked)
        rows.append(picked)
    loss = 1.0 / (1.0 + rows[0])
    source = jnp.where(lane == OUTSIDE, 0.0, COURANT * loss)
    return (source, rows[1] * loss, rows[2], rows[3])


def look_up(tables, cells):
    index = cells.astype(jnp.int32)
    return [jnp.take_along_axis(t, index, axis=1, mode="promise_in_bounds") for t in tables]


def cell_step(centre, around, older, state, source, weight, decay, couple):
    moved = source * (around + K0 * centre - K1 * older) - weight * state
    return older + moved, decay * state + couple * moved


def kernel(
    n_x, n_y,
    p_in, q_in, v_in, mask_in, mat_in, low_in, high_in, table,
    p_out, v_out,
    field_a, field_b, state_a, cls, coef, mask, mat,
    m_left, m_right, r_left, r_right,
    s_field_a, s_field_b, s_state_a, s_coef, s_ghost, edge,
    load_sem, send_sem, recv_sem,
):
    field, state = (field_a, field_b), (state_a,)
    s_field, s_state = (s_field_a, s_field_b), (s_state_a,)
    gx, gy = lax.axis_index("gx"), lax.axis_index("gy")

    def there(dx, dy):
        x, y = gx + dx, gy + dy
        return (x >= 0) & (x < n_x) & (y >= 0) & (y < n_y)

    around = [(dx, dy) for dx in (-1, 0, 1) for dy in (-1, 0, 1) if dx or dy]
    barrier = pltpu.get_barrier_semaphore()
    count = jnp.int32(0)
    for dx, dy in around:
        ok = there(dx, dy)
        count = count + ok.astype(jnp.int32)

        @pl.when(ok)
        def _():
            pl.semaphore_signal(barrier, inc=1, device_id=(gx + dx, gy + dy), device_id_type=MESH)

    own = pl.ds(2 * H, ROWS)
    loads = [
        pltpu.make_async_copy(src, dst, load_sem.at[i])
        for i, (src, dst) in enumerate(
            [
                (p_in, field[0].at[pl.ds(1, NZ), own]),
                (q_in, field[1].at[pl.ds(1, NZ), own]),
                (v_in, state[0].at[:, own]),
                (mask_in, mask),
                (mat_in, mat),
                (low_in, field[0].at[0, own]),
                (high_in, field[0].at[NZ + 1, own]),
            ]
        )
    ]
    for load in loads:
        load.start()

    lane = lane_ids()
    place = lane % 16
    tables = class_tables(table)
    for load in loads:
        load.wait()

    @pl.loop(0, NZ, unroll=7)
    def _(z):
        for k in range(4):
            rows = pl.ds(8 * k, 8)
            wall = mask[z, rows, :] == 1
            cls[z, pl.ds(16 + 8 * k, 8), :] = jnp.where(wall, mat[z, rows, :], AIR).astype(F32)

    def merge(bit, low, high):
        return jnp.where((lane & bit) != 0, high, low)

    def pack(out, first, spare, ghost_shift):
        def column(a, z, rows):
            ref, plane = ((field[0], z + 1), (field[1], z + 1), (state[0], z), (cls, z))[a]
            return ref[plane, rows, :]

        for j in range(PLANES):
            at = first + j + ghost_shift
            low_at, high_at = OFFSET[1] + spare, OFFSET[1] + 48 + spare
            for k in range(4):
                rows = pl.ds(16 + 8 * k, 8)
                parts = [
                    [roll(column(a, 7 * g + j, rows), OFFSET[a] + 16 * g - first) for g in range(GROUPS)]
                    for a in range(4)
                ]
                parts[1][0] = jnp.where(lane == low_at, roll(field[0][0, rows, :], low_at - at), parts[1][0])
                parts[1][3] = jnp.where(lane == high_at, roll(field[0][NZ + 1, rows, :], high_at - at), parts[1][3])
                halves = []
                for a in (0, 2):
                    g = [merge(8, parts[a][g], parts[a + 1][g]) for g in range(GROUPS)]
                    halves.append(merge(32, merge(16, g[0], g[1]), merge(16, g[2], g[3])))
                out[j, pl.ds(8 + 8 * k, 8), :] = merge(64, halves[0], halves[1])

    pack(m_left, 0, 7, 0)
    pack(m_right, LANES - 8, 0, 1)

    pl.semaphore_wait(barrier, count)

    transfers = []

    def transfer(src, dst, dx, dy):
        i = len(transfers)
        copy = pltpu.make_async_remote_copy(
            src_ref=src, dst_ref=dst, send_sem=send_sem.at[i], recv_sem=recv_sem.at[i],
            device_id=(gx + dx, gy + dy), device_id_type=MESH,
        )
        transfers.append((copy, dx, dy))

    for dx, message, into in ((1, m_right, r_left), (-1, m_left, r_right)):
        transfer(message.at[:, pl.ds(8, ROWS)], into.at[:, pl.ds(8, ROWS)], dx, 0)
    for dy, main_from, main_to, part_from, part_to in ((1, 40, 8, 32, 0), (-1, 16, 48, 8, 40)):
        for dx, message, into in ((1, m_right, r_left), (-1, m_left, r_right)):
            transfer(message.at[:, pl.ds(part_from, 8)], into.at[:, pl.ds(part_to, 8)], dx, dy)
        src, dst = pl.ds(main_from, 8), pl.ds(main_to, 8)
        transfer(field[0].at[:, src], field[0].at[:, dst], 0, dy)
        transfer(field[1].at[pl.ds(1, NZ), src], field[1].at[pl.ds(1, NZ), dst], 0, dy)
        transfer(state[0].at[:, src], state[0].at[:, dst], 0, dy)
        transfer(cls.at[:, src], cls.at[:, dst], 0, dy)
        for message in (m_left, m_right):
            transfer(message.at[:, pl.ds(part_from, 8)], message.at[:, pl.ds(part_to, 8)], 0, dy)

    for copy, dx, dy in transfers:

        @pl.when(there(dx, dy))
        def _():
            copy.start()

    nothing = jnp.where((lane >= 64) & (place >= 8), float(OUTSIDE), 0.0).astype(F32)

    def blank(ref, first, rows):
        @pl.loop(0, PLANES)
        def _(j):
            for k in range(rows // 8):
                ref[j, pl.ds(first + 8 * k, 8), :] = nothing

    for dy, main, part in ((-1, 8, 0), (1, 48, 40)):

        @pl.when(jnp.logical_not(there(0, dy)))
        def _():
            rows = pl.ds(main, 8)
            zero = jnp.zeros((8, LANES), F32)
            field[0][0, rows, :] = zero
            field[0][NZ + 1, rows, :] = zero

            @pl.loop(0, NZ)
            def _(z):
                field[0][z + 1, rows, :] = zero
                field[1][z + 1, rows, :] = zero
                state[0][z, rows, :] = zero
                cls[z, rows, :] = jnp.full((8, LANES), float(OUTSIDE), F32)

            blank(m_left, part, 8)
            blank(m_right, part, 8)

        for dx, ref in ((-1, r_left), (1, r_right)):

            @pl.when(there(dx, 0) & jnp.logical_not(there(0, dy)))
            def _():
                blank(ref, part, 8)

    for dx, ref in ((-1, r_left), (1, r_right)):

        @pl.when(jnp.logical_not(there(dx, 0)))
        def _():
            blank(ref, 0, TALL)

    def coefficients(blocks):
        @pl.loop(0, NZ, unroll=7)
        def _(z):
            for k in blocks:
                rows = pl.ds(8 + 8 * k, 8)
                for i, value in enumerate(look_up(tables, cls[z, rows, :])):
                    coef[i, z, rows, :] = value

    coefficients((1, 2, 3, 4))

    def receive(part):
        for copy, dx, dy in transfers:
            if (0 if dx == 0 else 1 if dy == 0 else 2) == part:

                @pl.when(there(-dx, -dy))
                def _():
                    copy.wait_recv()

    def gather_strip(a, j, rows):
        at = OFFSET[a]
        lower = merge(8, roll(r_left[j, rows, :], -at), roll(m_left[j, rows, :], 8 - at))
        upper = merge(8, roll(m_right[j, rows, :], 64 - at), roll(r_right[j, rows, :], 72 - at))
        return merge(64, lower, upper)

    def strips(blocks):
        @pl.loop(0, PLANES, unroll=7)
        def _(j):
            for k in blocks:
                rows, into = pl.ds(8 * k, 8), pl.ds(8 + 8 * k, 8)
                s_field[0][j + 1, into, :] = gather_strip(0, j, rows)
                s_field[1][j + 1, into, :] = gather_strip(1, j, rows)
                s_state[0][j, into, :] = gather_strip(2, j, rows)
                for i, value in enumerate(look_up(tables, gather_strip(3, j, rows))):
                    s_coef[i, j, into, :] = value

        for k in blocks:
            rows = pl.ds(8 * k, 8)
            total = jnp.zeros((8, LANES), F32)
            for j in range(PLANES):
                for ref, spare, to in ((r_left, 0, 1), (m_left, 7, 8), (m_right, 0, 65), (r_right, 7, 72)):
                    value = roll(ref[j, rows, :], to + j - OFFSET[1] - spare)
                    total = jnp.where((lane == to + j) | (lane == to + j + 48), value, total)
            s_ghost[pl.ds(8 + 8 * k, 8), :] = total

    receive(0)
    coefficients((0, 5))
    for k in range(6):
        rows = pl.ds(8 + 8 * k, 8)
        for plane in (0, NZ + 1):
            field[1][plane, rows, :] = field[0][plane, rows, :]
    receive(1)
    strips((1, 2, 3, 4))
    receive(2)
    strips((0, 5))

    group = (lane // 16) % 4

    def strip_ends(ref):
        for k in range(6):
            rows = pl.ds(8 + 8 * k, 8)
            ghost = s_ghost[rows, :]
            ref[0, rows, :] = jnp.where(group == 0, ghost, roll(ref[PLANES, rows, :], 16))
            ref[PLANES + 1, rows, :] = jnp.where(group == 3, ghost, roll(ref[1, rows, :], -16))

    strip_ends(s_field[0])
    mark = place == 6


    def y_sum(ref, plane, k):
        return ref[plane, pl.ds(7 + 8 * k, 8), :] + ref[plane, pl.ds(9 + 8 * k, 8), :]

    def strip_step(p, q, blocks):
        for j in range(PLANES):
            done = []
            for k in blocks:
                rows = pl.ds(8 + 8 * k, 8)
                centre = p[j + 1, rows, :]
                edge[j, rows, :] = jnp.where(mark, roll(centre, -66), centre)
                total = (roll(centre, 1) + roll(centre, -1)) + y_sum(p, j + 1, k) + (p[j, rows, :] + p[j + 2, rows, :])
                done.append((rows,) + cell_step(
                    centre, total, q[j + 1, rows, :], s_state[0][j, rows, :], *[s_coef[i, j, rows, :] for i in range(4)],
                ))
            for rows, newer, filt in done:
                q[j + 1, rows, :] = newer
                s_state[0][j, rows, :] = filt

    first_lane, last_lane = lane == 0, lane == LANES - 1

    def main_step(p, q, blocks, store):
        def group_step(g):
            shift = LANES - 7 - 16 * g
            for j in range(PLANES):
                z = 7 * g + j
                done = []
                for k in blocks:
                    rows = pl.ds(8 + 8 * k, 8)
                    centre = p[z + 1, rows, :]
                    beside = pltpu.roll(edge[j, rows, :], shift, axis=1)
                    total = (
                        (jnp.where(first_lane, beside, roll(centre, 1)) + jnp.where(last_lane, beside, roll(centre, -1)))
                        + y_sum(p, z + 1, k)
                        + (p[z, rows, :] + p[z + 2, rows, :])
                    )
                    done.append((k,) + cell_step(
                        centre, total, q[z + 1, rows, :], state[0][z, rows, :], *[coef[i, z, rows, :] for i in range(4)],
                    ))
                for k, newer, filt in done:
                    store(z, k, newer, filt)

        for g in range(GROUPS):
            group_step(g)

    every, inner = range(6), range(1, 5)

    def step(p, q, sp, sq):
        strip_step(sp, sq, every)
        strip_ends(sq)

        def store(z, k, newer, filt):
            rows = pl.ds(8 + 8 * k, 8)
            q[z + 1, rows, :] = newer
            state[0][z, rows, :] = filt

        main_step(p, q, every, store)

    for copy, dx, dy in transfers:

        @pl.when(there(dx, dy))
        def _():
            copy.wait_send()

    @pl.loop(0, ITERS // 2 - 1)
    def _(pair):
        step(field[0], field[1], s_field[0], s_field[1])
        step(field[1], field[0], s_field[1], s_field[0])

    step(field[0], field[1], s_field[0], s_field[1])
    strip_step(s_field[1], s_field[0], inner)

    def store_out(z, k, newer, filt):
        rows = pl.ds(8 * k - 8, 8)
        p_out[z, rows, :] = newer
        v_out[z, rows, :] = filt

    main_step(field[1], field[0], inner, store_out)


def solution(mesh):
    n_x, n_y = mesh.shape["gx"], mesh.shape["gy"]

    def body(*args):
        hbm = pl.BlockSpec(memory_space=pltpu.HBM)
        vmem = pl.BlockSpec(memory_space=pltpu.VMEM)
        big = (NZ, BUF, LANES)
        strip = (PLANES, BUF, LANES)
        message = pltpu.VMEM((PLANES, TALL, LANES), F32)
        tall, s_tall = (pltpu.VMEM((n + 2, BUF, LANES), F32) for n in (NZ, PLANES))
        n_transfers = 18
        return pl.pallas_call(
            lambda *refs: kernel(n_x, n_y, *refs),
            out_shape=[pltpu.VMEM((NZ, ROWS, LANES), F32)] * 2,
            in_specs=[hbm] * 7 + [pl.BlockSpec(memory_space=pltpu.SMEM)],
            out_specs=[vmem] * 2,
            scratch_shapes=[
                tall, tall,
                pltpu.VMEM(big, F32),
                pltpu.VMEM(big, F32),
                pltpu.VMEM((4,) + big, F32),
                pltpu.VMEM((NZ, ROWS, LANES), jnp.int32),
                pltpu.VMEM((NZ, ROWS, LANES), jnp.int32),
                message, message, message, message,
                s_tall, s_tall,
                pltpu.VMEM(strip, F32),
                pltpu.VMEM((4,) + strip, F32),
                pltpu.VMEM((BUF, LANES), F32),
                pltpu.VMEM(strip, F32),
                pltpu.SemaphoreType.DMA((7,)),
                pltpu.SemaphoreType.DMA((n_transfers,)),
                pltpu.SemaphoreType.DMA((n_transfers,)),
            ],
            compiler_params=pltpu.CompilerParams(
                collective_id=1, has_side_effects=True, vmem_limit_bytes=62 * 1024 * 1024
            ),
        )(*args)

    spec = P(None, "gy", "gx")
    return jax.shard_map(
        body,
        mesh=mesh,
        in_specs=(spec,) * 5 + (P("gy", "gx"),) * 2 + (P(),),
        out_specs=(spec, spec),
        check_vma=False,
    )
```

```python
import jax
import jax.numpy as jnp
from jax import lax
from jax.experimental import pallas as pl
from jax.experimental.pallas import tpu as pltpu
from jax.sharding import PartitionSpec as P

ITERS = 8
NZ = 28
ROWS = 32
LANES = 128
H = 8
GROUPS = 4
PLANES = 7
BUF = ROWS + 4 * H
TALL = ROWS + 2 * H
COURANT = 0.33
K0 = (2.0 - 6.0 * COURANT) / COURANT
K1 = 2.0 / COURANT
AIR = 8
OUTSIDE = 9
OFFSET = (0, 8, 64, 72)
MESH = pl.DeviceIdType.MESH
F32 = jnp.float32


def roll(value, shift):
    shift %= LANES
    return value if shift == 0 else pltpu.roll(value, shift, axis=1)


def lane_ids():
    return lax.broadcasted_iota(jnp.int32, (8, LANES), 1)


def class_tables(table):
    lane = lane_ids()
    rows = []
    for row, air in ((0, 0.0), (1, 0.0), (2, 1.0), (3, 0.0)):
        picked = jnp.full((8, LANES), air, F32)
        for index in range(8):
            picked = jnp.where(lane == index, table[row, index], picked)
        rows.append(picked)
    loss = 1.0 / (1.0 + rows[0])
    source = jnp.where(lane == OUTSIDE, 0.0, COURANT * loss)
    return (source, rows[1] * loss, rows[2], rows[3])


def look_up(tables, cells):
    index = cells.astype(jnp.int32)
    return [jnp.take_along_axis(t, index, axis=1, mode="promise_in_bounds") for t in tables]


def cell_step(centre, around, older, state, source, weight, decay, couple):
    moved = source * (around + K0 * centre - K1 * older) - weight * state
    return older + moved, decay * state + couple * moved


def kernel(
    n_x, n_y,
    p_in, q_in, v_in, mask_in, mat_in, low_in, high_in, table,
    p_out, v_out,
    field_a, field_b, state_a, cls, coef, mask, mat,
    m_left, m_right, r_left, r_right,
    s_field_a, s_field_b, s_state_a, s_coef, s_ghost, edge,
    load_sem, send_sem, recv_sem,
):
    field, state = (field_a, field_b), (state_a,)
    s_field, s_state = (s_field_a, s_field_b), (s_state_a,)
    gx, gy = lax.axis_index("gx"), lax.axis_index("gy")

    def there(dx, dy):
        x, y = gx + dx, gy + dy
        return (x >= 0) & (x < n_x) & (y >= 0) & (y < n_y)

    around = [(dx, dy) for dx in (-1, 0, 1) for dy in (-1, 0, 1) if dx or dy]
    barrier = pltpu.get_barrier_semaphore()
    count = jnp.int32(0)
    for dx, dy in around:
        ok = there(dx, dy)
        count = count + ok.astype(jnp.int32)

        @pl.when(ok)
        def _():
            pl.semaphore_signal(barrier, inc=1, device_id=(gx + dx, gy + dy), device_id_type=MESH)

    own = pl.ds(2 * H, ROWS)
    loads = [
        pltpu.make_async_copy(src, dst, load_sem.at[i])
        for i, (src, dst) in enumerate(
            [
                (p_in, field[0].at[pl.ds(1, NZ), own]),
                (q_in, field[1].at[pl.ds(1, NZ), own]),
                (v_in, state[0].at[:, own]),
                (mask_in, mask),
                (mat_in, mat),
                (low_in, field[0].at[0, own]),
                (high_in, field[0].at[NZ + 1, own]),
            ]
        )
    ]
    for load in loads:
        load.start()

    lane = lane_ids()
    place = lane % 16
    tables = class_tables(table)
    nothing = jnp.where((lane >= 64) & (place >= 8), float(OUTSIDE), 0.0).astype(F32)

    far = jnp.full((1, LANES), float(OUTSIDE), F32)
    none = jnp.zeros((1, LANES), F32)
    for z in range(NZ):
        for row in (8, 55):
            cls[z, pl.ds(row, 1), :] = far
            field[1][z + 1, pl.ds(row, 1), :] = none
            state[0][z, pl.ds(row, 1), :] = none
    for ref in (m_left, m_right, r_left, r_right):
        for j in range(PLANES):
            for row in (0, TALL - 1):
                ref[j, pl.ds(row, 1), :] = nothing[0:1]

    for load in loads:
        load.wait()

    @pl.loop(0, NZ, unroll=7)
    def _(z):
        for k in range(4):
            rows = pl.ds(8 * k, 8)
            wall = mask[z, rows, :] == 1
            cls[z, pl.ds(16 + 8 * k, 8), :] = jnp.where(wall, mat[z, rows, :], AIR).astype(F32)

    def merge(bit, low, high):
        return jnp.where((lane & bit) != 0, high, low)

    def pack(out, first, spare, ghost_shift):
        def column(a, z, rows):
            ref, plane = ((field[0], z + 1), (field[1], z + 1), (state[0], z), (cls, z))[a]
            return ref[plane, rows, :]

        for j in range(PLANES):
            at = first + j + ghost_shift
            low_at, high_at = OFFSET[1] + spare, OFFSET[1] + 48 + spare
            for k in range(4):
                rows = pl.ds(16 + 8 * k, 8)
                parts = [
                    [roll(column(a, 7 * g + j, rows), OFFSET[a] + 16 * g - first) for g in range(GROUPS)]
                    for a in range(4)
                ]
                parts[1][0] = jnp.where(lane == low_at, roll(field[0][0, rows, :], low_at - at), parts[1][0])
                parts[1][3] = jnp.where(lane == high_at, roll(field[0][NZ + 1, rows, :], high_at - at), parts[1][3])
                halves = []
                for a in (0, 2):
                    g = [merge(8, parts[a][g], parts[a + 1][g]) for g in range(GROUPS)]
                    halves.append(merge(32, merge(16, g[0], g[1]), merge(16, g[2], g[3])))
                out[j, pl.ds(8 + 8 * k, 8), :] = merge(64, halves[0], halves[1])

    pack(m_left, 0, 7, 0)
    pack(m_right, LANES - 8, 0, 1)

    pl.semaphore_wait(barrier, count)

    transfers = []

    def transfer(src, dst, dx, dy):
        i = len(transfers)
        copy = pltpu.make_async_remote_copy(
            src_ref=src, dst_ref=dst, send_sem=send_sem.at[i], recv_sem=recv_sem.at[i],
            device_id=(gx + dx, gy + dy), device_id_type=MESH,
        )
        transfers.append((copy, dx, dy))

    for dx, message, into in ((1, m_right, r_left), (-1, m_left, r_right)):
        transfer(message.at[:, pl.ds(8, ROWS)], into.at[:, pl.ds(8, ROWS)], dx, 0)
    for dy, main_from, main_to, part_from, part_to in ((1, 40, 8, 32, 0), (-1, 16, 48, 8, 40)):
        skip = 1 if dy > 0 else 0
        part_src, part_dst = pl.ds(part_from + skip, 7), pl.ds(part_to + skip, 7)
        for dx, message, into in ((1, m_right, r_left), (-1, m_left, r_right)):
            transfer(message.at[:, part_src], into.at[:, part_dst], dx, dy)
        src, dst = pl.ds(main_from + skip, 7), pl.ds(main_to + skip, 7)
        transfer(field[0].at[:, pl.ds(main_from, 8)], field[0].at[:, pl.ds(main_to, 8)], 0, dy)
        transfer(field[1].at[pl.ds(1, NZ), src], field[1].at[pl.ds(1, NZ), dst], 0, dy)
        transfer(state[0].at[:, src], state[0].at[:, dst], 0, dy)
        transfer(cls.at[:, src], cls.at[:, dst], 0, dy)
        for message in (m_left, m_right):
            transfer(message.at[:, part_src], message.at[:, part_dst], 0, dy)

    for copy, dx, dy in transfers:

        @pl.when(there(dx, dy))
        def _():
            copy.start()


    def blank(ref, first, rows):
        @pl.loop(0, PLANES)
        def _(j):
            for k in range(rows // 8):
                ref[j, pl.ds(first + 8 * k, 8), :] = nothing

    for dy, main, part in ((-1, 8, 0), (1, 48, 40)):

        @pl.when(jnp.logical_not(there(0, dy)))
        def _():
            rows = pl.ds(main, 8)
            zero = jnp.zeros((8, LANES), F32)
            field[0][0, rows, :] = zero
            field[0][NZ + 1, rows, :] = zero

            @pl.loop(0, NZ)
            def _(z):
                field[0][z + 1, rows, :] = zero
                field[1][z + 1, rows, :] = zero
                state[0][z, rows, :] = zero
                cls[z, rows, :] = jnp.full((8, LANES), float(OUTSIDE), F32)

            blank(m_left, part, 8)
            blank(m_right, part, 8)

        for dx, ref in ((-1, r_left), (1, r_right)):

            @pl.when(there(dx, 0) & jnp.logical_not(there(0, dy)))
            def _():
                blank(ref, part, 8)

    for dx, ref in ((-1, r_left), (1, r_right)):

        @pl.when(jnp.logical_not(there(dx, 0)))
        def _():
            blank(ref, 0, TALL)

    def coefficients(blocks):
        @pl.loop(0, NZ, unroll=7)
        def _(z):
            for k in blocks:
                rows = pl.ds(8 + 8 * k, 8)
                for i, value in enumerate(look_up(tables, cls[z, rows, :])):
                    coef[i, z, rows, :] = value

    coefficients((1, 2, 3, 4))

    def receive(part):
        for copy, dx, dy in transfers:
            if (0 if dx == 0 else 1 if dy == 0 else 2) == part:

                @pl.when(there(-dx, -dy))
                def _():
                    copy.wait_recv()

    def gather_strip(a, j, rows):
        at = OFFSET[a]
        lower = merge(8, roll(r_left[j, rows, :], -at), roll(m_left[j, rows, :], 8 - at))
        upper = merge(8, roll(m_right[j, rows, :], 64 - at), roll(r_right[j, rows, :], 72 - at))
        return merge(64, lower, upper)

    def strips(blocks):
        @pl.loop(0, PLANES, unroll=7)
        def _(j):
            for k in blocks:
                rows, into = pl.ds(8 * k, 8), pl.ds(8 + 8 * k, 8)
                s_field[0][j + 1, into, :] = gather_strip(0, j, rows)
                s_field[1][j + 1, into, :] = gather_strip(1, j, rows)
                s_state[0][j, into, :] = gather_strip(2, j, rows)
                for i, value in enumerate(look_up(tables, gather_strip(3, j, rows))):
                    s_coef[i, j, into, :] = value

        for k in blocks:
            rows = pl.ds(8 * k, 8)
            total = jnp.zeros((8, LANES), F32)
            for j in range(PLANES):
                for ref, spare, to in ((r_left, 0, 1), (m_left, 7, 8), (m_right, 0, 65), (r_right, 7, 72)):
                    value = roll(ref[j, rows, :], to + j - OFFSET[1] - spare)
                    total = jnp.where((lane == to + j) | (lane == to + j + 48), value, total)
            s_ghost[pl.ds(8 + 8 * k, 8), :] = total

    receive(0)
    coefficients((0, 5))
    for k in range(6):
        rows = pl.ds(8 + 8 * k, 8)
        for plane in (0, NZ + 1):
            field[1][plane, rows, :] = field[0][plane, rows, :]
    receive(1)
    strips((1, 2, 3, 4))
    receive(2)
    strips((0, 5))

    group = (lane // 16) % 4

    def strip_ends(ref):
        for k in range(6):
            rows = pl.ds(8 + 8 * k, 8)
            ghost = s_ghost[rows, :]
            ref[0, rows, :] = jnp.where(group == 0, ghost, roll(ref[PLANES, rows, :], 16))
            ref[PLANES + 1, rows, :] = jnp.where(group == 3, ghost, roll(ref[1, rows, :], -16))

    strip_ends(s_field[0])
    mark = place == 6


    def y_sum(ref, plane, k):
        return ref[plane, pl.ds(7 + 8 * k, 8), :] + ref[plane, pl.ds(9 + 8 * k, 8), :]

    def strip_step(p, q, blocks):
        for j in range(PLANES):
            done = []
            for k in blocks:
                rows = pl.ds(8 + 8 * k, 8)
                centre = p[j + 1, rows, :]
                edge[j, rows, :] = jnp.where(mark, roll(centre, -66), centre)
                total = (roll(centre, 1) + roll(centre, -1)) + y_sum(p, j + 1, k) + (p[j, rows, :] + p[j + 2, rows, :])
                done.append((rows,) + cell_step(
                    centre, total, q[j + 1, rows, :], s_state[0][j, rows, :], *[s_coef[i, j, rows, :] for i in range(4)],
                ))
            for rows, newer, filt in done:
                q[j + 1, rows, :] = newer
                s_state[0][j, rows, :] = filt

    first_lane, last_lane = lane == 0, lane == LANES - 1

    def main_step(p, q, blocks, store):
        def group_step(g):
            shift = LANES - 7 - 16 * g
            for j in range(PLANES):
                z = 7 * g + j
                done = []
                for k in blocks:
                    rows = pl.ds(8 + 8 * k, 8)
                    centre = p[z + 1, rows, :]
                    beside = pltpu.roll(edge[j, rows, :], shift, axis=1)
                    total = (
                        (jnp.where(first_lane, beside, roll(centre, 1)) + jnp.where(last_lane, beside, roll(centre, -1)))
                        + y_sum(p, z + 1, k)
                        + (p[z, rows, :] + p[z + 2, rows, :])
                    )
                    done.append((k,) + cell_step(
                        centre, total, q[z + 1, rows, :], state[0][z, rows, :], *[coef[i, z, rows, :] for i in range(4)],
                    ))
                for k, newer, filt in done:
                    store(z, k, newer, filt)

        for g in range(GROUPS):
            group_step(g)

    every, inner = range(6), range(1, 5)

    def step(p, q, sp, sq):
        strip_step(sp, sq, every)
        strip_ends(sq)

        def store(z, k, newer, filt):
            rows = pl.ds(8 + 8 * k, 8)
            q[z + 1, rows, :] = newer
            state[0][z, rows, :] = filt

        main_step(p, q, every, store)

    for copy, dx, dy in transfers:

        @pl.when(there(dx, dy))
        def _():
            copy.wait_send()

    @pl.loop(0, ITERS // 2 - 1)
    def _(pair):
        step(field[0], field[1], s_field[0], s_field[1])
        step(field[1], field[0], s_field[1], s_field[0])

    step(field[0], field[1], s_field[0], s_field[1])
    strip_step(s_field[1], s_field[0], inner)

    def store_out(z, k, newer, filt):
        rows = pl.ds(8 * k - 8, 8)
        p_out[z, rows, :] = newer
        v_out[z, rows, :] = filt

    main_step(field[1], field[0], inner, store_out)


def solution(mesh):
    n_x, n_y = mesh.shape["gx"], mesh.shape["gy"]

    def body(*args):
        hbm = pl.BlockSpec(memory_space=pltpu.HBM)
        vmem = pl.BlockSpec(memory_space=pltpu.VMEM)
        big = (NZ, BUF, LANES)
        strip = (PLANES, BUF, LANES)
        message = pltpu.VMEM((PLANES, TALL, LANES), F32)
        tall, s_tall = (pltpu.VMEM((n + 2, BUF, LANES), F32) for n in (NZ, PLANES))
        n_transfers = 18
        return pl.pallas_call(
            lambda *refs: kernel(n_x, n_y, *refs),
            out_shape=[pltpu.VMEM((NZ, ROWS, LANES), F32)] * 2,
            in_specs=[hbm] * 7 + [pl.BlockSpec(memory_space=pltpu.SMEM)],
            out_specs=[vmem] * 2,
            scratch_shapes=[
                tall, tall,
                pltpu.VMEM(big, F32),
                pltpu.VMEM(big, F32),
                pltpu.VMEM((4,) + big, F32),
                pltpu.VMEM((NZ, ROWS, LANES), jnp.int32),
                pltpu.VMEM((NZ, ROWS, LANES), jnp.int32),
                message, message, message, message,
                s_tall, s_tall,
                pltpu.VMEM(strip, F32),
                pltpu.VMEM((4,) + strip, F32),
                pltpu.VMEM((BUF, LANES), F32),
                pltpu.VMEM(strip, F32),
                pltpu.SemaphoreType.DMA((7,)),
                pltpu.SemaphoreType.DMA((n_transfers,)),
                pltpu.SemaphoreType.DMA((n_transfers,)),
            ],
            compiler_params=pltpu.CompilerParams(
                collective_id=1, has_side_effects=True, vmem_limit_bytes=62 * 1024 * 1024
            ),
        )(*args)

    spec = P(None, "gy", "gx")
    return jax.shard_map(
        body,
        mesh=mesh,
        in_specs=(spec,) * 5 + (P("gy", "gx"),) * 2 + (P(),),
        out_specs=(spec, spec),
        check_vma=False,
    )
```

```python
import jax
import jax.numpy as jnp
from jax import lax
from jax.experimental import pallas as pl
from jax.experimental.pallas import tpu as pltpu
from jax.sharding import PartitionSpec as P

ITERS = 8
NZ = 28
ROWS = 32
LANES = 128
H = 8
GROUPS = 4
PLANES = 7
BUF = ROWS + 4 * H
TALL = ROWS + 2 * H
COURANT = 0.33
K0 = (2.0 - 6.0 * COURANT) / COURANT
K1 = 2.0 / COURANT
AIR = 8
OUTSIDE = 9
OFFSET = (0, 8, 64, 72)
MESH = pl.DeviceIdType.MESH
F32 = jnp.float32


def roll(value, shift):
    shift %= LANES
    return value if shift == 0 else pltpu.roll(value, shift, axis=1)


def lane_ids():
    return lax.broadcasted_iota(jnp.int32, (8, LANES), 1)


def class_tables(table):
    lane = lane_ids()
    rows = []
    for row, air in ((0, 0.0), (1, 0.0), (2, 1.0), (3, 0.0)):
        picked = jnp.full((8, LANES), air, F32)
        for index in range(8):
            picked = jnp.where(lane == index, table[row, index], picked)
        rows.append(picked)
    loss = 1.0 / (1.0 + rows[0])
    source = jnp.where(lane == OUTSIDE, 0.0, COURANT * loss)
    return (source, rows[1] * loss, rows[2], rows[3])


def look_up(tables, cells):
    index = cells.astype(jnp.int32)
    return [jnp.take_along_axis(t, index, axis=1, mode="promise_in_bounds") for t in tables]


def cell_step(centre, around, older, state, source, weight, decay, couple):
    moved = source * (around + K0 * centre - K1 * older) - weight * state
    return older + moved, decay * state + couple * moved


def kernel(
    n_x, n_y,
    p_in, q_in, v_in, mask_in, mat_in, low_in, high_in, table,
    p_out, v_out,
    field_a, field_b, state_a, cls, coef, mask, mat,
    m_left, m_right, r_left, r_right,
    s_field_a, s_field_b, s_state_a, s_coef, s_ghost, edge,
    load_sem, send_sem, recv_sem,
):
    field, state = (field_a, field_b), (state_a,)
    s_field, s_state = (s_field_a, s_field_b), (s_state_a,)
    gx, gy = lax.axis_index("gx"), lax.axis_index("gy")

    def there(dx, dy):
        x, y = gx + dx, gy + dy
        return (x >= 0) & (x < n_x) & (y >= 0) & (y < n_y)

    around = [(dx, dy) for dx in (-1, 0, 1) for dy in (-1, 0, 1) if dx or dy]
    barrier = pltpu.get_barrier_semaphore()
    count = jnp.int32(0)
    for dx, dy in around:
        ok = there(dx, dy)
        count = count + ok.astype(jnp.int32)

        @pl.when(ok)
        def _():
            pl.semaphore_signal(barrier, inc=1, device_id=(gx + dx, gy + dy), device_id_type=MESH)

    own = pl.ds(2 * H, ROWS)
    loads = [
        pltpu.make_async_copy(src, dst, load_sem.at[i])
        for i, (src, dst) in enumerate(
            [
                (mask_in, mask),
                (mat_in, mat),
                (p_in, field[0].at[pl.ds(1, NZ), own]),
                (q_in, field[1].at[pl.ds(1, NZ), own]),
                (v_in, state[0].at[:, own]),
                (low_in, field[0].at[0, own]),
                (high_in, field[0].at[NZ + 1, own]),
            ]
        )
    ]
    for load in loads:
        load.start()

    lane = lane_ids()
    place = lane % 16
    tables = class_tables(table)
    nothing = jnp.where((lane >= 64) & (place >= 8), float(OUTSIDE), 0.0).astype(F32)

    far = jnp.full((1, LANES), float(OUTSIDE), F32)
    none = jnp.zeros((1, LANES), F32)
    for z in range(NZ):
        for row in (8, 55):
            cls[z, pl.ds(row, 1), :] = far
            field[1][z + 1, pl.ds(row, 1), :] = none
            state[0][z, pl.ds(row, 1), :] = none
    for ref in (m_left, m_right, r_left, r_right):
        for j in range(PLANES):
            for row in (0, TALL - 1):
                ref[j, pl.ds(row, 1), :] = nothing[0:1]

    for load in loads[:2]:
        load.wait()

    @pl.loop(0, NZ, unroll=7)
    def _(z):
        for k in range(4):
            rows = pl.ds(8 * k, 8)
            wall = mask[z, rows, :] == 1
            cls[z, pl.ds(16 + 8 * k, 8), :] = jnp.where(wall, mat[z, rows, :], AIR).astype(F32)

    for load in loads[2:]:
        load.wait()

    def merge(bit, low, high):
        return jnp.where((lane & bit) != 0, high, low)

    def pack(out, first, spare, ghost_shift):
        def column(a, z, rows):
            ref, plane = ((field[0], z + 1), (field[1], z + 1), (state[0], z), (cls, z))[a]
            return ref[plane, rows, :]

        for j in range(PLANES):
            at = first + j + ghost_shift
            low_at, high_at = OFFSET[1] + spare, OFFSET[1] + 48 + spare
            for k in range(4):
                rows = pl.ds(16 + 8 * k, 8)
                parts = [
                    [roll(column(a, 7 * g + j, rows), OFFSET[a] + 16 * g - first) for g in range(GROUPS)]
                    for a in range(4)
                ]
                parts[1][0] = jnp.where(lane == low_at, roll(field[0][0, rows, :], low_at - at), parts[1][0])
                parts[1][3] = jnp.where(lane == high_at, roll(field[0][NZ + 1, rows, :], high_at - at), parts[1][3])
                halves = []
                for a in (0, 2):
                    g = [merge(8, parts[a][g], parts[a + 1][g]) for g in range(GROUPS)]
                    halves.append(merge(32, merge(16, g[0], g[1]), merge(16, g[2], g[3])))
                out[j, pl.ds(8 + 8 * k, 8), :] = merge(64, halves[0], halves[1])

    pack(m_left, 0, 7, 0)
    pack(m_right, LANES - 8, 0, 1)

    pl.semaphore_wait(barrier, count)

    transfers = []

    def transfer(src, dst, dx, dy):
        i = len(transfers)
        copy = pltpu.make_async_remote_copy(
            src_ref=src, dst_ref=dst, send_sem=send_sem.at[i], recv_sem=recv_sem.at[i],
            device_id=(gx + dx, gy + dy), device_id_type=MESH,
        )
        transfers.append((copy, dx, dy))

    for dx, message, into in ((1, m_right, r_left), (-1, m_left, r_right)):
        transfer(message.at[:, pl.ds(8, ROWS)], into.at[:, pl.ds(8, ROWS)], dx, 0)
    for dy, main_from, main_to, part_from, part_to in ((1, 40, 8, 32, 0), (-1, 16, 48, 8, 40)):
        skip = 1 if dy > 0 else 0
        part_src, part_dst = pl.ds(part_from + skip, 7), pl.ds(part_to + skip, 7)
        for dx, message, into in ((1, m_right, r_left), (-1, m_left, r_right)):
            transfer(message.at[:, part_src], into.at[:, part_dst], dx, dy)
        src, dst = pl.ds(main_from + skip, 7), pl.ds(main_to + skip, 7)
        transfer(field[0].at[:, pl.ds(main_from, 8)], field[0].at[:, pl.ds(main_to, 8)], 0, dy)
        transfer(field[1].at[pl.ds(1, NZ), src], field[1].at[pl.ds(1, NZ), dst], 0, dy)
        transfer(state[0].at[:, src], state[0].at[:, dst], 0, dy)
        transfer(cls.at[:, src], cls.at[:, dst], 0, dy)
        for message in (m_left, m_right):
            transfer(message.at[:, part_src], message.at[:, part_dst], 0, dy)

    for copy, dx, dy in transfers:

        @pl.when(there(dx, dy))
        def _():
            copy.start()


    def blank(ref, first, rows):
        @pl.loop(0, PLANES)
        def _(j):
            for k in range(rows // 8):
                ref[j, pl.ds(first + 8 * k, 8), :] = nothing

    for dy, main, part in ((-1, 8, 0), (1, 48, 40)):

        @pl.when(jnp.logical_not(there(0, dy)))
        def _():
            rows = pl.ds(main, 8)
            zero = jnp.zeros((8, LANES), F32)
            field[0][0, rows, :] = zero
            field[0][NZ + 1, rows, :] = zero

            @pl.loop(0, NZ)
            def _(z):
                field[0][z + 1, rows, :] = zero
                field[1][z + 1, rows, :] = zero
                state[0][z, rows, :] = zero
                cls[z, rows, :] = jnp.full((8, LANES), float(OUTSIDE), F32)

            blank(m_left, part, 8)
            blank(m_right, part, 8)

        for dx, ref in ((-1, r_left), (1, r_right)):

            @pl.when(there(dx, 0) & jnp.logical_not(there(0, dy)))
            def _():
                blank(ref, part, 8)

    for dx, ref in ((-1, r_left), (1, r_right)):

        @pl.when(jnp.logical_not(there(dx, 0)))
        def _():
            blank(ref, 0, TALL)

    def coefficients(blocks):
        @pl.loop(0, NZ, unroll=7)
        def _(z):
            for k in blocks:
                rows = pl.ds(8 + 8 * k, 8)
                for i, value in enumerate(look_up(tables, cls[z, rows, :])):
                    coef[i, z, rows, :] = value

    coefficients((1, 2, 3, 4))

    def receive(part):
        for copy, dx, dy in transfers:
            if (0 if dx == 0 else 1 if dy == 0 else 2) == part:

                @pl.when(there(-dx, -dy))
                def _():
                    copy.wait_recv()

    def gather_strip(a, j, rows):
        at = OFFSET[a]
        lower = merge(8, roll(r_left[j, rows, :], -at), roll(m_left[j, rows, :], 8 - at))
        upper = merge(8, roll(m_right[j, rows, :], 64 - at), roll(r_right[j, rows, :], 72 - at))
        return merge(64, lower, upper)

    def strips(blocks):
        @pl.loop(0, PLANES, unroll=7)
        def _(j):
            for k in blocks:
                rows, into = pl.ds(8 * k, 8), pl.ds(8 + 8 * k, 8)
                s_field[0][j + 1, into, :] = gather_strip(0, j, rows)
                s_field[1][j + 1, into, :] = gather_strip(1, j, rows)
                s_state[0][j, into, :] = gather_strip(2, j, rows)
                for i, value in enumerate(look_up(tables, gather_strip(3, j, rows))):
                    s_coef[i, j, into, :] = value

        for k in blocks:
            rows = pl.ds(8 * k, 8)
            total = jnp.zeros((8, LANES), F32)
            for j in range(PLANES):
                for ref, spare, to in ((r_left, 0, 1), (m_left, 7, 8), (m_right, 0, 65), (r_right, 7, 72)):
                    value = roll(ref[j, rows, :], to + j - OFFSET[1] - spare)
                    total = jnp.where((lane == to + j) | (lane == to + j + 48), value, total)
            s_ghost[pl.ds(8 + 8 * k, 8), :] = total

    receive(0)
    coefficients((0, 5))
    for k in range(6):
        rows = pl.ds(8 + 8 * k, 8)
        for plane in (0, NZ + 1):
            field[1][plane, rows, :] = field[0][plane, rows, :]
    receive(1)
    strips((1, 2, 3, 4))
    receive(2)
    strips((0, 5))

    group = (lane // 16) % 4

    def strip_ends(ref):
        for k in range(6):
            rows = pl.ds(8 + 8 * k, 8)
            ghost = s_ghost[rows, :]
            ref[0, rows, :] = jnp.where(group == 0, ghost, roll(ref[PLANES, rows, :], 16))
            ref[PLANES + 1, rows, :] = jnp.where(group == 3, ghost, roll(ref[1, rows, :], -16))

    strip_ends(s_field[0])
    mark = place == 6


    def y_sum(ref, plane, k):
        return ref[plane, pl.ds(7 + 8 * k, 8), :] + ref[plane, pl.ds(9 + 8 * k, 8), :]

    def strip_step(p, q, blocks):
        for j in range(PLANES):
            done = []
            for k in blocks:
                rows = pl.ds(8 + 8 * k, 8)
                centre = p[j + 1, rows, :]
                edge[j, rows, :] = jnp.where(mark, roll(centre, -66), centre)
                total = (roll(centre, 1) + roll(centre, -1)) + y_sum(p, j + 1, k) + (p[j, rows, :] + p[j + 2, rows, :])
                done.append((rows,) + cell_step(
                    centre, total, q[j + 1, rows, :], s_state[0][j, rows, :], *[s_coef[i, j, rows, :] for i in range(4)],
                ))
            for rows, newer, filt in done:
                q[j + 1, rows, :] = newer
                s_state[0][j, rows, :] = filt

    first_lane, last_lane = lane == 0, lane == LANES - 1

    def main_step(p, q, blocks, store):
        def group_step(g):
            shift = LANES - 7 - 16 * g
            for j in range(PLANES):
                z = 7 * g + j
                done = []
                for k in blocks:
                    rows = pl.ds(8 + 8 * k, 8)
                    centre = p[z + 1, rows, :]
                    beside = pltpu.roll(edge[j, rows, :], shift, axis=1)
                    total = (
                        (jnp.where(first_lane, beside, roll(centre, 1)) + jnp.where(last_lane, beside, roll(centre, -1)))
                        + y_sum(p, z + 1, k)
                        + (p[z, rows, :] + p[z + 2, rows, :])
                    )
                    done.append((k,) + cell_step(
                        centre, total, q[z + 1, rows, :], state[0][z, rows, :], *[coef[i, z, rows, :] for i in range(4)],
                    ))
                for k, newer, filt in done:
                    store(z, k, newer, filt)

        for g in range(GROUPS):
            group_step(g)

    every, inner = range(6), range(1, 5)

    def step(p, q, sp, sq):
        strip_step(sp, sq, every)
        strip_ends(sq)

        def store(z, k, newer, filt):
            rows = pl.ds(8 + 8 * k, 8)
            q[z + 1, rows, :] = newer
            state[0][z, rows, :] = filt

        main_step(p, q, every, store)

    for copy, dx, dy in transfers:

        @pl.when(there(dx, dy))
        def _():
            copy.wait_send()

    @pl.loop(0, ITERS // 2 - 1)
    def _(pair):
        step(field[0], field[1], s_field[0], s_field[1])
        step(field[1], field[0], s_field[1], s_field[0])

    step(field[0], field[1], s_field[0], s_field[1])
    strip_step(s_field[1], s_field[0], inner)

    def store_out(z, k, newer, filt):
        rows = pl.ds(8 * k - 8, 8)
        p_out[z, rows, :] = newer
        v_out[z, rows, :] = filt

    main_step(field[1], field[0], inner, store_out)


def solution(mesh):
    n_x, n_y = mesh.shape["gx"], mesh.shape["gy"]

    def body(*args):
        hbm = pl.BlockSpec(memory_space=pltpu.HBM)
        vmem = pl.BlockSpec(memory_space=pltpu.VMEM)
        big = (NZ, BUF, LANES)
        strip = (PLANES, BUF, LANES)
        message = pltpu.VMEM((PLANES, TALL, LANES), F32)
        tall, s_tall = (pltpu.VMEM((n + 2, BUF, LANES), F32) for n in (NZ, PLANES))
        n_transfers = 18
        return pl.pallas_call(
            lambda *refs: kernel(n_x, n_y, *refs),
            out_shape=[pltpu.VMEM((NZ, ROWS, LANES), F32)] * 2,
            in_specs=[hbm] * 7 + [pl.BlockSpec(memory_space=pltpu.SMEM)],
            out_specs=[vmem] * 2,
            scratch_shapes=[
                tall, tall,
                pltpu.VMEM(big, F32),
                pltpu.VMEM(big, F32),
                pltpu.VMEM((4,) + big, F32),
                pltpu.VMEM((NZ, ROWS, LANES), jnp.int32),
                pltpu.VMEM((NZ, ROWS, LANES), jnp.int32),
                message, message, message, message,
                s_tall, s_tall,
                pltpu.VMEM(strip, F32),
                pltpu.VMEM((4,) + strip, F32),
                pltpu.VMEM((BUF, LANES), F32),
                pltpu.VMEM(strip, F32),
                pltpu.SemaphoreType.DMA((7,)),
                pltpu.SemaphoreType.DMA((n_transfers,)),
                pltpu.SemaphoreType.DMA((n_transfers,)),
            ],
            compiler_params=pltpu.CompilerParams(
                collective_id=1, has_side_effects=True, vmem_limit_bytes=62 * 1024 * 1024
            ),
        )(*args)

    spec = P(None, "gy", "gx")
    return jax.shard_map(
        body,
        mesh=mesh,
        in_specs=(spec,) * 5 + (P("gy", "gx"),) * 2 + (P(),),
        out_specs=(spec, spec),
        check_vma=False,
    )
```
